256 devices in a mesh: vert: 16 (over x_lo, z), off: 16 (over x_hi, y, core).
Axes of the slice: x: 4 (x_hi: 2, x_lo: 2; x = x_hi * 2 + x_lo), y: 4, z: 8, core: 2. Of those that a mesh axis runs over, the one named last changes fastest.
Arguments:
- features: bfloat16 [32768, 256], P(('vert', 'off')), may hold values from -16 to 16
- norm_gain: float32 [256], replicated, may hold values from 0.25 to 1.75
- w_query: bfloat16 [256, 256], replicated, may hold values from -1 to 1
- w_keyval: bfloat16 [256, 512], replicated, may hold values from -1 to 1
- w_out: bfloat16 [256, 256], replicated, may hold values from -0.375 to 0.375
- project: bfloat16 [1024, 16384], P(None, ('vert', 'off')), may hold values from -0.1875 to 0.1875
- hub_rows: int32 [16384], P(('vert', 'off')), may hold values from 0 to 127
- expander_shift: int32 [3], replicated, may hold values from 0 to 127
- local_edges: int32 [32768, 16], P(('vert', 'off')), may hold values from 0 to 127
- cotangent: bfloat16 [32768, 256], P(('vert', 'off')), may hold values from -6 to 6
Outputs:
- mixed: bfloat16 [32768, 256], P(('vert', 'off'))
- grad_features: float32 [32768, 256], P(('vert', 'off'))
- grad_gain: float32 [256], replicated
- grad_query: float32 [256, 256], replicated
- grad_keyval: float32 [256, 512], replicated
- grad_out: float32 [256, 256], replicated
The draws below stay inside these ranges and needn't reach their ends.
Inputs may be any that keep to these rules, and one draw needn't show every extreme that they name: `hub_rows`: entries are rows of a block. `local_edges`: entries are rows of a block. `expander_shift`: entries are row offsets within a block.
All inputs are finite; a program needn't handle non-finite values.
Results may differ from the reference program's by a relative error of at most 0.0039.
The reference program's roundings to bfloat16 on the way count: a program that leaves them out, or rounds other values in their place, can miss the bound.
Values may be sent and summed in bfloat16 or wider, within the bound.
No kernel may reach another device: no remote copies, remote signals or barrier semaphores. Data moves between devices by JAX's collectives and lax.ppermute only.
A program may use at most 128 MiB of HBM per device.

```python
import jax
import jax.numpy as jnp
from jax import lax

D = 256
HEADS = 8
LAND = 1024
VDEV = 128
HUB_DEV = 64
DEG = 16
NV = 32768
NHUB = 16384
N_VERT = 16
N_OFF = 16


def draw_features(key, part):
    key = jax.random.fold_in(key, 1)
    noise = jax.random.truncated_normal(jax.random.fold_in(key, 2), -6.0, 6.0, (NV, D), jnp.float32)
    return noise.astype(jnp.bfloat16)


def draw_w_query(key, part):
    key = jax.random.fold_in(key, 5)
    base = jax.random.truncated_normal(key, -6.0, 6.0, (D, D), jnp.float32) * D ** (-0.5)
    return base.astype(jnp.bfloat16)


def draw_w_keyval(key, part):
    key = jax.random.fold_in(key, 6)
    base = jax.random.truncated_normal(key, -6.0, 6.0, (D, 2 * D), jnp.float32) * D ** (-0.5)
    return base.astype(jnp.bfloat16)


def touch_ends(values, own_key, least, top_value):
    shape = values.shape
    index_at = [jax.random.randint(jax.random.fold_in(own_key, axis), (), 0, shape[axis]) for axis in range(len(shape))]
    values = values.at[tuple(index_at)].set(least)
    longest = shape.index(max(shape))
    index_at[longest] = (index_at[longest] + 1) % shape[longest]
    return values.at[tuple(index_at)].set(top_value)


def raised(result, stream_key, source, target, parts, factor):
    owner, partner = [(jnp.arange(result.shape[axis_at]) // (result.shape[axis_at] // parts)).reshape([-1 if axis == axis_at else 1 for axis in range(result.ndim)]) for axis_at in (source, target)]
    chosen = jax.random.permutation(stream_key, parts)[partner]
    strong = (owner == chosen) | (owner == (partner + parts // 2) % parts)
    return jnp.where(strong, factor * result, result)


def block_levels(own_key, dims, cuts, least, largest):
    loudness, own = 1.0, jax.random.fold_in(own_key, 6)
    for dim, shards_of in cuts:
        steps = jnp.exp(jax.random.uniform(jax.random.fold_in(own, dim), (shards_of,), jnp.float32, least / len(cuts), largest / len(cuts)))
        loudness = loudness * jnp.repeat(steps, dims[dim] // shards_of).reshape([-1 if axis == dim else 1 for axis in range(len(dims))])
    return loudness


def scatter_about(key, dims, width, most, cuts=(), held_as=jnp.bfloat16):
    array = width * jax.random.normal(key, dims, jnp.float32)
    if cuts:
        array = array * block_levels(key, dims, cuts, -0.22, 0.18)
    return jnp.clip(array, -most, most).astype(held_as)


def gaussian_with(stream_key, shape, spread, limit, cuts, heavy, held_as=jnp.bfloat16):
    entries = spread * jax.random.normal(stream_key, shape, jnp.float32)
    if cuts:
        entries = entries * block_levels(stream_key, shape, cuts, -0.22, 0.18)
    return jnp.clip(raised(entries, jax.random.fold_in(stream_key, 3), *heavy), -limit, limit).astype(held_as)


def setup_inputs(seed: int = 0) -> dict:
    streams_of = jax.random.split(jax.random.key(seed), 11)
    features = draw_features(jax.random.fold_in(streams_of[10], 71), 0)
    norm_gain = jnp.clip(1.0 + 0.15 * jax.random.normal(streams_of[1], (D,), jnp.float32), 0.25, 1.75)
    w_query = draw_w_query(jax.random.fold_in(streams_of[10], 71), 0)
    w_keyval = draw_w_keyval(jax.random.fold_in(streams_of[10], 71), 0)
    w_out = scatter_about(streams_of[4], (D, D), D ** -0.5, 0.375)
    project = gaussian_with(streams_of[5], (LAND, NHUB), NHUB ** -0.5, 0.1875, ((1, 256),), (1, 0, 256, 6.0))
    hub_rows = touch_ends(jax.random.randint(streams_of[6], (NHUB,), 0, VDEV), jax.random.fold_in(streams_of[6], 1), 0, VDEV - 1).astype(jnp.int32)
    expander_shift = jax.random.randint(streams_of[7], (3,), 0, VDEV).astype(jnp.int32)
    local_edges = touch_ends(jax.random.randint(streams_of[8], (NV, DEG), 0, VDEV), jax.random.fold_in(streams_of[8], 1), 0, VDEV - 1).astype(jnp.int32)
    cotangent = scatter_about(streams_of[9], (NV, D), 1.0, 6.0, ((0, 256),))
    return dict(features=features, norm_gain=norm_gain, w_query=w_query, w_keyval=w_keyval, w_out=w_out, project=project, hub_rows=hub_rows, expander_shift=expander_shift, local_edges=local_edges, cotangent=cotangent)


def norm_rows(floats, gain):
    meansq = lax.optimization_barrier(jnp.mean(floats * floats, axis=-1, keepdims=True))
    return floats * lax.rsqrt(meansq + 1e-06) * gain

def attend_block(queries_f, extra_rows, landmark):
    row_count = queries_f.shape[0]
    feature_width = queries_f.shape[1]
    head_size = feature_width // HEADS
    queries = queries_f.reshape(row_count, HEADS, head_size) * head_size ** (-0.5)
    extra = extra_rows.astype(jnp.float32)
    ext_keys = extra[..., :feature_width].reshape(row_count, -1, HEADS, head_size)
    ext_values = extra[..., feature_width:].reshape(row_count, -1, HEADS, head_size)
    land_keys = landmark[:, :feature_width].reshape(-1, HEADS, head_size)
    land_values = landmark[:, feature_width:].reshape(-1, HEADS, head_size)
    s_land = jnp.einsum('vhd,lhd->vhl', queries, land_keys, precision=lax.Precision.HIGHEST)
    s_ext = jnp.einsum('vhd,vehd->vhe', queries, ext_keys, precision=lax.Precision.HIGHEST)
    highest = lax.stop_gradient(jnp.maximum(s_land.max(-1), s_ext.max(-1)))[..., None]
    p_land = jnp.exp(s_land - highest)
    p_ext = jnp.exp(s_ext - highest)
    total = p_land.sum(-1) + p_ext.sum(-1)
    weighted = jnp.einsum('vhl,lhd->vhd', p_land, land_values, precision=lax.Precision.HIGHEST) + jnp.einsum('vhe,vehd->vhd', p_ext, ext_values, precision=lax.Precision.HIGHEST)
    return (weighted / total[..., None]).reshape(row_count, feature_width)

def reference(features, norm_gain, w_query, w_keyval, w_out, project, hub_rows, expander_shift, local_edges, cotangent):
    blocks = N_VERT * N_OFF
    shifts = (1, -1, N_OFF // 2)
    start_rows = (jnp.arange(blocks, dtype=jnp.int32) * VDEV)[:, None]
    hub_index = (hub_rows.reshape(blocks, HUB_DEV).astype(jnp.int32) + start_rows).reshape(-1)
    edge_blocks = local_edges.reshape(blocks, VDEV, DEG).astype(jnp.int32)

    def forward(floats, gain_in, weight_query, weight_keyval, weight_out):
        normed = norm_rows(floats, gain_in).astype(jnp.bfloat16)
        normed_f = lax.optimization_barrier(normed).astype(jnp.float32)
        query = jnp.dot(normed_f, weight_query, precision=lax.Precision.HIGHEST).astype(jnp.bfloat16)
        keyval = jnp.dot(normed_f, weight_keyval, precision=lax.Precision.HIGHEST).astype(jnp.bfloat16)
        query, keyval = lax.optimization_barrier((query, keyval))
        hub_keys = jnp.dot(normed_f[hub_index], weight_keyval, precision=lax.Precision.HIGHEST)
        landmark = jnp.dot(project.astype(jnp.float32), hub_keys, precision=lax.Precision.HIGHEST)
        layout = keyval.reshape(N_VERT, N_OFF, VDEV, 2 * D)
        nears = tuple((jnp.roll(layout, amount, axis=1).reshape(blocks, VDEV, 2 * D) for amount in shifts))

        @jax.checkpoint
        def one_block(pieces):
            query_part, keyval_part, near_part, edge_part = pieces
            rolled = jnp.stack([jnp.roll(near_one, -expander_shift[idx], axis=0) for idx, near_one in enumerate(near_part)], axis=1)
            extra = jnp.concatenate([rolled, keyval_part[edge_part]], axis=1)
            return attend_block(query_part.astype(jnp.float32), extra, landmark)
        attended = lax.map(one_block, (query.reshape(blocks, VDEV, D), keyval.reshape(blocks, VDEV, 2 * D), nears, edge_blocks))
        attended = attended.reshape(NV, D).astype(jnp.bfloat16)
        attended_f = lax.optimization_barrier(attended).astype(jnp.float32)
        return (floats + jnp.dot(attended_f, weight_out, precision=lax.Precision.HIGHEST)).astype(jnp.bfloat16)
    mixed, pull_back = jax.vjp(forward, features.astype(jnp.float32), norm_gain, w_query.astype(jnp.float32), w_keyval.astype(jnp.float32), w_out.astype(jnp.float32))
    grad_x, grad_g, grad_q, grad_kv, grad_o = pull_back(cotangent)
    return (mixed, grad_x, grad_g, grad_q, grad_kv, grad_o)
```

```python
import jax
import jax.numpy as jnp
import numpy as np
from jax import lax
from jax.experimental import pallas as pl
from jax.experimental.pallas import tpu as pltpu
from jax.sharding import Mesh, PartitionSpec as P

F32 = jnp.float32
BF16 = jnp.bfloat16
HEADS = 8
VMEM_LIMIT = 48 * 1024 * 1024

VERT = ("xl", "z")
OFF = ("xh", "y", "c")
EVERY = VERT + OFF
PLANE = ("xl", "xh", "y")


def dot(a, b, ca, cb):
    return lax.dot_general(a, b, (((ca,), (cb,)), ((), ())), preferred_element_type=F32)


def split(x):
    hi = x.astype(BF16)
    return hi, (x - hi.astype(F32)).astype(BF16)


def columns_of(index_row, count):
    n = index_row.shape[1]
    return (lax.broadcasted_iota(jnp.int32, (count, n), 0) == index_row).astype(BF16)


def normalised(x, gain):
    x = x.astype(F32)
    scale = lax.rsqrt(jnp.mean(x * x, axis=-1, keepdims=True) + 1e-06)
    return (x * scale * gain).astype(BF16)


def front_kernel(core_ref, x_ref, gain_ref, project_ref, hubs_ref, normed_ref, part_ref):
    normed = normalised(x_ref[...], gain_ref[...])
    normed_ref[...] = normed
    hub = dot(columns_of(hubs_ref[...], normed.shape[0]), normed, 0, 0).astype(BF16)
    half = part_ref.shape[1]
    core = core_ref[0]
    for slot in range(2):
        which = core if slot == 0 else 1 - core
        rows = project_ref[:, pl.ds(pl.multiple_of(which * half, half), half)]
        part_ref[slot] = dot(rows, hub, 0, 0)


def main_kernel(
    core_ref,
    shift_ref,
    x_ref,
    cot_ref,
    gain_ref,
    normed_ref,
    inside_ref,
    cross_ref,
    far_ref,
    sum_mine_ref,
    sum_other_ref,
    edges_ref,
    wq_ref,
    wkv_ref,
    wo_ref,
    mixed_ref,
    sums_ref,
    dq_ref,
    dkv_ref,
    back_inside_ref,
    back_cross_ref,
    back_far_ref,
    rows_ref,
    k_ref,
    v_ref,
    kt_ref,
    vt_ref,
    k_low_ref,
    v_low_ref,
    kt_low_ref,
    vt_low_ref,
    p_ref,
    ds_ref,
    grads_ref,
):
    n, width = x_ref.shape
    half = sum_mine_ref.shape[0]
    land = 2 * half
    keys = land + n
    size = width // HEADS
    scale = size ** (-0.5)
    core = core_ref[0]
    first = jnp.broadcast_to(core, (n, width)) == 0
    inside = inside_ref[...].astype(F32)
    cross = cross_ref[...].astype(F32)
    nears = (
        jnp.where(first, cross, inside).astype(BF16),
        jnp.where(first, inside, cross).astype(BF16),
        far_ref[...],
    )
    backs = []

    first_half = jnp.broadcast_to(core, (half, width)) == 0
    sum_mine = sum_mine_ref[...]
    sum_other = sum_other_ref[...]
    top_hi, top_lo = split(jnp.where(first_half, sum_mine, sum_other))
    end_hi, end_lo = split(jnp.where(first_half, sum_other, sum_mine))
    rows_ref[0:half, :] = top_hi
    rows_ref[half:land, :] = end_hi
    land_lo = jnp.concatenate([top_lo, end_lo], axis=0)
    normed = normed_ref[...]
    rows_ref[land:keys, :] = normed
    at_row = lax.broadcasted_iota(jnp.int32, (n, n), 0)
    at_col = lax.broadcasted_iota(jnp.int32, (n, n), 1)
    rolls = []
    for e in range(3):
        target = at_row + shift_ref[e]
        target = jnp.where(target >= n, target - n, target)
        rolls.append((at_col == target).astype(BF16))
        rolled = dot(rolls[e], nears[e], 1, 0)
        rows_ref[keys + e * n : keys + (e + 1) * n, :] = normalised(rolled, gain_ref[...])

    wkv = wkv_ref[...]
    wkv_t = wkv.astype(F32).T.astype(BF16)
    base = rows_ref[0:keys, :]
    keyval = dot(base, wkv, 1, 0)
    land_hi, land_low = split(keyval[:land] + dot(land_lo, wkv, 1, 0))
    own = keyval[land:].astype(BF16)
    for at, cols in ((0, slice(0, width)), (1, slice(width, 2 * width))):
        (k_ref, v_ref)[at][0:land, :] = land_hi[:, cols]
        (k_ref, v_ref)[at][land:keys, :] = own[:, cols]
        (k_low_ref, v_low_ref)[at][...] = land_low[:, cols]
    keyval_t = dot(wkv_t, base, 1, 1)
    land_hi, land_low = split(keyval_t[:, :land] + dot(wkv_t, land_lo, 1, 1))
    own = keyval_t[:, land:].astype(BF16)
    for at, rows in ((0, slice(0, width)), (1, slice(width, 2 * width))):
        (kt_ref, vt_ref)[at][:, 0:land] = land_hi[rows]
        (kt_ref, vt_ref)[at][:, land:keys] = own[rows]
        (kt_low_ref, vt_low_ref)[at][...] = land_low[rows]
    near_t = dot(wkv_t, rows_ref[keys : keys + 3 * n, :], 1, 1).astype(BF16).astype(F32)
    q = dot(normed, wq_ref[...], 1, 0).astype(BF16)
    q_f = q.astype(F32)
    qt = q_f.T
    cot = cot_ref[...]
    wo = wo_ref[...]
    do = dot(cot, wo, 1, 1).astype(BF16)
    do_f = do.astype(F32)
    dot_t = do_f.T

    kts = [near_t[:width, e * n : (e + 1) * n] for e in range(3)]
    vts = [near_t[width:, e * n : (e + 1) * n] for e in range(3)]
    s_near = [(qt * kt).reshape(HEADS, size, n).sum(1) * scale for kt in kts]
    dp_near = [(dot_t * vt).reshape(HEADS, size, n).sum(1) for vt in vts]

    counts = jnp.zeros((n, n), F32)
    for i in range(edges_ref.shape[0]):
        counts = counts + (at_row == edges_ref[i : i + 1, :]).astype(F32)
    counts = jnp.concatenate([counts, counts], axis=1)
    present = counts > 0.0

    qq = jnp.concatenate([q_f, q_f], axis=0)
    dodo = jnp.concatenate([do_f, do_f], axis=0)
    qqt = jnp.concatenate([qt, qt], axis=1)
    dodot = jnp.concatenate([dot_t, dot_t], axis=1)
    pair_row = lax.broadcasted_iota(jnp.int32, (2 * n, width), 0) // n
    pair_head = lax.broadcasted_iota(jnp.int32, (2 * n, width), 1) // size
    pair_row_t = lax.broadcasted_iota(jnp.int32, (width, 2 * n), 1) // n
    pair_head_t = lax.broadcasted_iota(jnp.int32, (width, 2 * n), 0) // size
    q_stack = []
    do_stack = []
    out_t = []
    dq_t = []
    tops = []
    inverses = []
    deltas = []

    def pair_of(a, j):
        return jnp.concatenate([a[2 * j : 2 * j + 1], a[2 * j + 1 : 2 * j + 2]], axis=1)

    for j in range(HEADS // 2):
        mine = pair_head == 2 * j + pair_row
        mine_t = pair_head_t == 2 * j + pair_row_t
        q_stack.append(jnp.where(mine, qq, 0.0).astype(BF16))
        do_stack.append(jnp.where(mine, dodo, 0.0).astype(BF16))
        q_sel = jnp.where(mine_t, qqt, 0.0).astype(BF16)
        do_sel = jnp.where(mine_t, dodot, 0.0).astype(BF16)
        s = dot(k_ref[...], q_sel, 1, 0)
        s_land = (s[:land] + dot(k_low_ref[...], q_sel, 1, 0)) * scale
        s_loc = jnp.where(present, s[land:] * scale, -1e30)
        sn = [pair_of(a, j) for a in s_near]
        dpn = [pair_of(a, j) for a in dp_near]
        top = jnp.maximum(s_land.max(0, keepdims=True), s_loc.max(0, keepdims=True))
        for a in sn:
            top = jnp.maximum(top, a)
        p_land = jnp.exp(s_land - top)
        p_loc = counts * jnp.exp(s_loc - top)
        pn = [jnp.exp(a - top) for a in sn]
        total = p_land.sum(0, keepdims=True) + p_loc.sum(0, keepdims=True) + (pn[0] + pn[1] + pn[2])
        inverse = 1.0 / total
        dp = dot(v_ref[...], do_sel, 1, 0)
        dp_land = dp[:land] + dot(v_low_ref[...], do_sel, 1, 0)
        dp_loc = dp[land:]
        p_land = p_land * inverse
        p_loc = p_loc * inverse
        delta = (p_land * dp_land).sum(0, keepdims=True) + (p_loc * dp_loc).sum(0, keepdims=True)
        for a, b in zip(pn, dpn):
            delta = delta + a * inverse * b
        lanes = slice(2 * n * j, 2 * n * (j + 1))
        p_hi, p_lo = split(jnp.concatenate([p_land, p_loc], axis=0))
        p_ref[:, lanes] = p_hi
        ds_land = p_land * (dp_land - delta)
        ds_hi, ds_lo = split(jnp.concatenate([ds_land, p_loc * (dp_loc - delta)], axis=0))
        ds_ref[:, lanes] = ds_hi
        head_rows = slice(2 * size * j, 2 * size * (j + 1))
        o = dot(vt_ref[head_rows, :], p_hi, 1, 0) + dot(vt_ref[head_rows, :], p_lo, 1, 0)
        o = o + dot(vt_low_ref[head_rows, :], p_hi[:land], 1, 0)
        out_t += [o[:size, :n], o[size:, n:]]
        g = dot(kt_ref[head_rows, :], ds_hi, 1, 0) + dot(kt_ref[head_rows, :], ds_lo, 1, 0)
        g = g + dot(kt_low_ref[head_rows, :], ds_hi[:land], 1, 0)
        dq_t += [g[:size, :n], g[size:, n:]]
        for held, value in ((tops, top), (inverses, inverse), (deltas, delta)):
            held += [value[:, :n], value[:, n:]]

    out_t = jnp.concatenate(out_t, axis=0)
    dq_t = jnp.concatenate(dq_t, axis=0)
    top = jnp.concatenate(tops, axis=0)
    inverse = jnp.concatenate(inverses, axis=0)
    delta = jnp.concatenate(deltas, axis=0)

    def spread(a):
        return jnp.broadcast_to(a[:, None, :], (HEADS, size, n)).reshape(width, n)

    for e in range(3):
        p = jnp.exp(s_near[e] - top) * inverse
        ds = p * (dp_near[e] - delta)
        p_all = spread(p)
        ds_all = spread(ds)
        out_t = out_t + p_all * vts[e]
        dq_t = dq_t + ds_all * kts[e]
        back = jnp.concatenate([ds_all * scale * qt, p_all * dot_t], axis=0).T.astype(BF16)
        grads_ref[keys + e * n : keys + (e + 1) * n, :] = back
        backs.append(dot(rolls[e], back, 0, 0))

    first = jnp.broadcast_to(core, backs[0].shape) == 0
    back_inside_ref[...] = jnp.where(first, backs[1], backs[0]).astype(BF16)
    back_cross_ref[...] = jnp.where(first, backs[0], backs[1]).astype(BF16)
    back_far_ref[...] = backs[2].astype(BF16)

    attended_t = out_t.astype(BF16)
    attended = attended_t.astype(F32).T.astype(BF16)
    mixed_ref[...] = (x_ref[...].astype(F32) + dot(attended, wo, 1, 0)).astype(BF16)
    dq = (dq_t * scale).T.astype(BF16)
    dq_ref[...] = dq

    dk = dot(ds_ref[...], jnp.concatenate(q_stack, axis=0), 1, 0) * scale
    dv = dot(p_ref[...], jnp.concatenate(do_stack, axis=0), 1, 0)
    dland = jnp.concatenate([dk[:land], dv[:land]], axis=1)
    dkv = jnp.concatenate([dk[land:], dv[land:]], axis=1).astype(BF16)
    dkv_ref[...] = dkv
    dland_hi, dland_lo = split(dland)
    grads_ref[0:land, :] = dland_hi
    grads_ref[land:keys, :] = dkv

    sums_ref[core] = dot(dland_hi, wkv, 1, 1) + dot(dland_lo, wkv, 1, 1)
    other = 1 - core
    sums_ref[other, 0:width] = dot(normed, dq, 0, 0)
    dwkv = dot(rows_ref[...], grads_ref[...], 0, 0) + dot(rows_ref[0:land, :], dland_lo, 0, 0)
    sums_ref[other, width : 2 * width] = dwkv[:, :width]
    sums_ref[other, 2 * width : 3 * width] = dwkv[:, width:]
    sums_ref[other, 3 * width : 4 * width] = dot(attended_t, cot, 1, 0)


def tail_kernel(
    core_ref,
    x_ref,
    gain_ref,
    cot_ref,
    project_ref,
    hubs_ref,
    dq_ref,
    dkv_ref,
    inside_ref,
    cross_ref,
    far_ref,
    mine_ref,
    other_ref,
    wq_ref,
    wkv_ref,
    gx_ref,
    gg_ref,
    gq_ref,
    gkv_ref,
    go_ref,
):
    n, width = x_ref.shape
    first = jnp.broadcast_to(core_ref[0], mine_ref.shape) == 0
    mine = mine_ref[...].astype(F32)
    other = other_ref[...].astype(F32)
    land_sum = jnp.where(first, mine, other).astype(BF16)
    weights = jnp.where(first, other, mine)
    gain = gain_ref[...]
    wq = wq_ref[...]
    wkv = wkv_ref[...]

    gq = weights[0:width]
    gk = weights[width : 2 * width]
    gv = weights[2 * width : 3 * width]
    gq_ref[...] = gq
    gkv_ref[:, :width] = gk
    gkv_ref[:, width:] = gv
    go_ref[...] = weights[3 * width : 4 * width]
    both = gq * wq.astype(F32) + gk * wkv[:, :width].astype(F32) + gv * wkv[:, width:].astype(F32)
    gg_ref[...] = both.T.sum(0, keepdims=True) / gain

    dkv = dkv_ref[...]
    inside = inside_ref[...].astype(F32)
    cross = cross_ref[...].astype(F32)
    first = jnp.broadcast_to(core_ref[0], inside.shape) == 0
    pieces = (jnp.where(first, inside, cross), jnp.where(first, cross, inside), far_ref[...].astype(F32))
    for piece in pieces:
        dkv = (dkv.astype(F32) + piece).astype(BF16)
    dhub = dot(project_ref[...], land_sum, 1, 0)
    spread = columns_of(hubs_ref[...], n)
    dhub_hi, dhub_lo = split(dhub)
    dn = dot(dq_ref[...], wq, 1, 1) + dot(dkv, wkv, 1, 1)
    dn = dn + (dot(spread, dhub_hi, 1, 0) + dot(spread, dhub_lo, 1, 0))
    dn = dn.astype(BF16).astype(F32) * gain
    x = x_ref[...].astype(F32)
    scale = lax.rsqrt(jnp.mean(x * x, axis=-1, keepdims=True) + 1e-06)
    along = jnp.mean(dn * x, axis=-1, keepdims=True)
    gx_ref[...] = scale * dn - x * (scale * scale * scale * along) + cot_ref[...].astype(F32)


def call(kernel, outs, scratch, smem, *args):
    where = [pl.BlockSpec(memory_space=pltpu.SMEM)] * smem
    where += [pl.BlockSpec(memory_space=pltpu.VMEM)] * (len(args) - smem)
    return pl.pallas_call(
        kernel,
        out_shape=[jax.ShapeDtypeStruct(*o) for o in outs],
        in_specs=where,
        out_specs=[pl.BlockSpec(memory_space=pltpu.VMEM)] * len(outs),
        scratch_shapes=[pltpu.VMEM(*s) for s in scratch],
        compiler_params=pltpu.CompilerParams(vmem_limit_bytes=VMEM_LIMIT),
    )(*args)


def across(value):
    return lax.ppermute(value, "c", [(0, 1), (1, 0)])


def exchange(values):
    count = lax.axis_size(OFF)
    between = [(o, (o + 1 if o % 2 else o - 1) % count) for o in range(count)]
    far = [(o, (o + count // 2) % count) for o in range(count)]
    inside, cross, away = values
    return (
        across(inside),
        lax.ppermute(cross, OFF, between),
        lax.ppermute(away, OFF, far),
    )


def sum_all(parts, beside, plane_type, deep_type, out_type):
    _, rows, width = parts.shape
    plane = lax.axis_size(PLANE)
    deep = lax.axis_size("z")
    held = parts[0] + across(parts[1])
    held = held.astype(plane_type).reshape(plane, rows // plane, width)
    held = lax.all_to_all(held, PLANE, 0, 0)
    held, beside = lax.optimization_barrier((held, beside))
    held = held.astype(F32).sum(0).astype(deep_type)
    held = jnp.broadcast_to(held[None], (deep,) + held.shape)
    held = lax.all_to_all(held, "z", 0, 0).astype(F32).sum(0).astype(out_type)
    held = jnp.broadcast_to(held[None], (plane,) + held.shape)
    held = lax.all_to_all(held, PLANE, 0, 0).reshape(rows, width)
    return held, across(held), beside


def shards(
    features,
    norm_gain,
    w_query,
    w_keyval,
    w_out,
    project,
    hub_rows,
    expander_shift,
    local_edges,
    cotangent,
):
    n, width = features.shape
    land, hubs = project.shape
    core = lax.axis_index("c").astype(jnp.int32).reshape(1)
    gain = norm_gain.reshape(1, width)
    project_t = project.T
    hub_row = hub_rows.reshape(1, hubs)
    nears = exchange((features, features, features))

    normed, part = call(
        front_kernel,
        [((n, width), BF16), ((2, land // 2, width), F32)],
        [],
        1,
        core,
        features,
        gain,
        project_t,
        hub_row,
    )
    sum_mine, sum_other, nears = sum_all(part, nears, F32, F32, F32)

    keys = land + n
    mixed, parts, dq, dkv, *backs = call(
        main_kernel,
        [
            ((n, width), BF16),
            ((2, land, width), F32),
            ((n, width), BF16),
            ((n, 2 * width), BF16),
            ((n, 2 * width), BF16),
            ((n, 2 * width), BF16),
            ((n, 2 * width), BF16),
        ],
        [
            ((keys + 3 * n, width), BF16),
            ((keys, width), BF16),
            ((keys, width), BF16),
            ((width, keys), BF16),
            ((width, keys), BF16),
            ((land, width), BF16),
            ((land, width), BF16),
            ((width, land), BF16),
            ((width, land), BF16),
            ((keys, HEADS * n), BF16),
            ((keys, HEADS * n), BF16),
            ((keys + 3 * n, 2 * width), BF16),
        ],
        2,
        core,
        expander_shift,
        features,
        cotangent,
        gain,
        normed,
        *nears,
        sum_mine,
        sum_other,
        local_edges.T,
        w_query,
        w_keyval,
        w_out,
    )
    pieces = exchange(backs)
    mine, other, pieces = sum_all(parts, pieces, BF16, F32, BF16)
    grad_x, grad_g, grad_q, grad_kv, grad_o = call(
        tail_kernel,
        [
            ((n, width), F32),
            ((1, width), F32),
            ((width, width), F32),
            ((width, 2 * width), F32),
            ((width, width), F32),
        ],
        [],
        1,
        core,
        features,
        gain,
        cotangent,
        project_t,
        hub_row,
        dq,
        dkv,
        *pieces,
        mine,
        other,
        w_query,
        w_keyval,
    )
    return mixed, grad_x, grad_g.reshape(width), grad_q, grad_kv, grad_o


def solution(mesh):
    fine = Mesh(np.asarray(mesh.devices).reshape(2, 8, 2, 4, 2), EVERY)
    placed = (
        P(EVERY, None),
        P(),
        P(),
        P(),
        P(),
        P(None, EVERY),
        P(EVERY),
        P(),
        P(EVERY, None),
        P(EVERY, None),
    )
    return jax.shard_map(
        shards,
        mesh=fine,
        in_specs=placed,
        out_specs=(P(EVERY, None), P(EVERY, None), P(), P(), P(), P()),
        check_vma=False,
    )
```
